32 devices in a mesh: grp: 2 (over y), blk: 4 (over z), fac: 4 (over x, core).
Axes of the slice: x: 2, y: 2, z: 4, core: 2. Of those that a mesh axis runs over, the one named last changes fastest.
Arguments:
- train_grads: bfloat16 [4096, 8192], P(('grp', 'blk')), parts along dimension 0, may hold values from -0.0625 to 0.0625
- queries: bfloat16 [2048, 8192], P(('grp', 'fac'), 'blk'), parts along dimension 0, may hold values from -6 to 6
- factor: bfloat16 [8192, 8192], P('blk', 'fac'), may hold values from -0.0625 to 0.0625
Outputs:
- scores: float32 [4096, 1024], P(('grp', 'blk'), 'fac'), parts along dimension 0
The draws below stay inside these ranges and needn't reach their ends.
There are 2 independent parts, one for each index of `grp`. The reference program is written for one: setup_inputs(seed, part) draws one part's arguments, and reference() takes and returns one part's arrays. A program takes and returns all parts, laid end to end along the dimension named above; an argument that names none is the same for every part. Nothing has to cross between parts.
All inputs are finite; a program needn't handle non-finite values.
Results may differ from the reference program's by a relative error of at most 0.009.
Values may be sent and summed in bfloat16 or wider, within the bound.
A program may use at most 128 MiB of HBM per device.

```python
import jax
import jax.numpy as jnp
from jax import lax

K = 8192
QUERIES = 1024
TRAIN = 2048
N_BLK = 4


def level_of(key, extent, split, low, top_value):
    level = 1.0
    for dim, parts in split:
        draws = jax.random.uniform(jax.random.fold_in(jax.random.fold_in(key, 6), dim), (parts,), jnp.float32, low / len(split), top_value / len(split))
        level = level * jnp.repeat(jnp.exp(draws), extent[dim] // parts).reshape((-1,) + (1,) * (len(extent) - 1 - dim))
    return level


def centred(rng, shape, scale, reach, pieces=(), dtype=jnp.bfloat16):
    loudness = level_of(rng, shape, pieces, -0.22, 0.18) if pieces else 1.0
    entries = jax.random.normal(rng, shape, jnp.float32) * scale * loudness
    return jnp.minimum(jnp.maximum(entries, -reach), reach).astype(dtype)


def setup_inputs(seed: int = 0, part: int = 0) -> dict:
    seeds = jax.random.split(jax.random.key(seed), 4)
    own_keys = jax.random.split(jax.random.fold_in(seeds[3], part), 4)
    return {
        "train_grads": centred(own_keys[0], (TRAIN, K), K ** -0.5, 0.0625, ((0, 4),)),
        "queries": centred(own_keys[1], (QUERIES, K), 1.0, 6.0, ((0, 4), (1, 4))),
        "factor": centred(seeds[2], (K, K), K ** -0.5, 0.0625, ((0, 4), (1, 4))),
    }


def reference(train_grads, queries, factor):
    mixed_rows = jnp.dot(queries, factor.T, preferred_element_type=jnp.float32).astype(jnp.bfloat16)
    width = K // N_BLK

    def block_term(block_index, summed):
        offset = (block_index * width)
        row_slab = lax.dynamic_slice_in_dim(mixed_rows, offset, width, 1)
        weights = lax.dynamic_slice_in_dim(factor, offset, width, 0)
        rounded = jnp.dot(row_slab, weights, preferred_element_type=jnp.float32).astype(jnp.bfloat16)
        rounded = lax.optimization_barrier(rounded)
        return summed + rounded.astype(jnp.float32)

    summed = lax.fori_loop(0, N_BLK, block_term, jnp.zeros((QUERIES, K), jnp.float32))
    precond = summed.astype(jnp.bfloat16)
    return jnp.dot(train_grads, precond.T, preferred_element_type=jnp.float32)
```

```python
import functools

import jax
import jax.numpy as jnp
from jax import lax
from jax.experimental import pallas as pl
from jax.experimental.pallas import tpu as pltpu
from jax.sharding import PartitionSpec as P

MESH = pl.DeviceIdType.MESH
CORES = 2
STEP_ROWS = 128
TILE_ROWS = 256
HOP = 2
CHUNK = 128

contract_last = functools.partial(
    lax.dot_general,
    dimension_numbers=(((1,), (1,)), ((), ())),
    preferred_element_type=jnp.float32,
)


def at_multiple(start, size):
    return pl.ds(pl.multiple_of(start, size), size)


def remote(src, dst, sems, index, target):
    send_sems, recv_sems = sems
    return pltpu.make_async_remote_copy(
        src_ref=src,
        dst_ref=dst,
        send_sem=send_sems.at[index],
        recv_sem=recv_sems.at[index],
        device_id=target,
        device_id_type=MESH,
    )


def meet(targets):
    barrier = pltpu.get_barrier_semaphore()
    for target in targets:
        pl.semaphore_signal(barrier, inc=1, device_id=target, device_id_type=MESH)
    pl.semaphore_wait(barrier, len(targets))


def term_kernel(
    n_blk, n_fac, queries, factor, term, all_queries, rows, total,
    local_sems, q_send, q_recv, x_send, x_recv, y_send, y_recv, o_send, o_recv, c_send, c_recv,
):
    grp, blk, fac = lax.axis_index("grp"), lax.axis_index("blk"), lax.axis_index("fac")
    chips = n_fac // CORES
    chip, core = fac // CORES, fac % CORES
    n_rows, width = factor.shape
    q_width = queries.shape[1]
    steps, half = n_rows // STEP_ROWS, STEP_ROWS // 2
    q_sems, x_sems, y_sems, o_sems, c_sems = (
        (q_send, q_recv), (x_send, x_recv), (y_send, y_recv), (o_send, o_recv), (c_send, c_recv)
    )

    def other_chip(distance):
        return (chip + distance + chips) % chips * CORES + core

    across = {"grp": 1 - grp}
    beside = {"fac": chip * CORES + 1 - core}
    meet(
        [across, beside]
        + [{"fac": other_chip(distance)} for distance in range(1, chips)]
        + [{"blk": (blk + 1) % n_blk}, {"blk": (blk + n_blk - 1) % n_blk}]
    )

    def region(start, size, owner):
        return rows.at[at_multiple(start, size), at_multiple(owner * width, width)]

    def own_half(step):
        return step * STEP_ROWS + grp * half

    def x_copy(step, distance, source):
        start = own_half(step)
        return remote(
            factor.at[at_multiple(start, half), :],
            region(start, half, source),
            x_sems,
            (distance - 1) * steps + step,
            {"fac": other_chip(distance)},
        )

    def y_copy(step, distance, which):
        part = region(step * STEP_ROWS + which * half, half, other_chip(-distance))
        return remote(part, part, y_sems, (distance - 1) * steps + step, across)

    def o_copy(step, owner):
        start = step * STEP_ROWS
        return remote(
            factor.at[at_multiple(start, STEP_ROWS), :],
            region(start, STEP_ROWS, owner),
            o_sems,
            step,
            beside,
        )

    def c_copy(step, distance, owner):
        part = region(step * STEP_ROWS, STEP_ROWS, owner)
        return remote(part, part, c_sems, (distance - 1) * steps + step, beside)

    def q_part(owner):
        return all_queries.at[:, at_multiple(owner * q_width, q_width)]

    def q_copy(owner, up):
        to = blk + 1 if up else blk - 1
        src = q_part(owner)
        return remote(src, src, q_sems, owner, {"blk": to})

    def q_send_own(up):
        to = blk + 1 if up else blk - 1
        return pltpu.make_async_remote_copy(
            src_ref=queries,
            dst_ref=q_part(blk),
            send_sem=q_send.at[n_blk if up else n_blk + 1],
            recv_sem=q_recv.at[blk],
            device_id={"blk": to},
            device_id_type=MESH,
        )

    keep_rows = pltpu.make_async_copy(factor, region(0, n_rows, fac), local_sems.at[0])
    keep_queries = pltpu.make_async_copy(queries, q_part(blk), local_sems.at[1])

    pl.when(blk < n_blk - 1)(lambda: q_send_own(True).start())
    pl.when(blk > 0)(lambda: q_send_own(False).start())
    ahead = min(3, steps)
    for step in range(ahead):
        for distance in range(1, chips):
            x_copy(step, distance, fac).start()
    keep_queries.start()
    keep_rows.start()

    def relay_queries(far):
        @pl.when(blk - far >= 0)
        def _():
            q_copy(blk - far, True).wait_recv()
            pl.when(blk < n_blk - 1)(lambda: q_copy(blk - far, True).start())

        @pl.when(blk + far <= n_blk - 1)
        def _():
            q_copy(blk + far, False).wait_recv()
            pl.when(blk > 0)(lambda: q_copy(blk + far, False).start())

    def multiply(tile, first, last):
        here = at_multiple(tile * TILE_ROWS, TILE_ROWS)
        depth = all_queries.shape[1]
        piece = min(2048, depth)

        def part(k, sums):
            cols = at_multiple(k * piece, piece)
            return sums + contract_last(all_queries[:, cols], rows[here, cols])

        zero = jnp.zeros((all_queries.shape[0], TILE_ROWS), jnp.float32)
        mixed = lax.fori_loop(0, depth // piece, part, zero).astype(jnp.bfloat16)
        wide = min(1024, depth)

        @pl.loop(0, depth // wide)
        def _(k):
            cols = at_multiple(k * wide, wide)
            sums = jnp.dot(mixed, rows[here, cols], preferred_element_type=jnp.float32)
            if not first:
                sums = sums + total[:, cols]
            if last:
                term[:, cols] = sums.astype(term.dtype)
            else:
                total[:, cols] = sums

    tiles, per_tile = n_rows // TILE_ROWS, TILE_ROWS // STEP_ROWS
    turns = steps + 2
    begin = turns * 3 // 4 - 1
    done = 0
    for turn in range(turns):
        if turn < steps:
            o_copy(turn, fac).start()
            for distance in range(1, chips):
                x_copy(turn, distance, other_chip(-distance)).wait_recv()
                y_copy(turn, distance, grp).start()
        if 1 <= turn <= steps:
            for distance in range(1, chips):
                y_copy(turn - 1, distance, 1 - grp).wait_recv()
                c_copy(turn - 1, distance, other_chip(-distance)).start()
        if turn < steps:
            for distance in range(1, chips):
                x_copy(turn, distance, fac).wait_send()
                if turn + ahead < steps:
                    x_copy(turn + ahead, distance, fac).start()
        for far in range(1, n_blk):
            if far * begin // (n_blk - 1) == turn:
                relay_queries(far)
        if turn == begin:
            keep_queries.wait()
            keep_rows.wait()
        if turn >= begin:
            allowed = tiles if turn == turns - 1 else min(done + 2, (turn - 1) // per_tile, tiles)
            while done < allowed:
                for step in range(done * per_tile, (done + 1) * per_tile):
                    o_copy(step, fac + 1 - 2 * core).wait_recv()
                    for distance in range(1, chips):
                        c_copy(step, distance, other_chip(-distance) + 1 - 2 * core).wait_recv()
                multiply(done, done == 0, done == tiles - 1)
                done += 1

    pl.when(blk < n_blk - 1)(lambda: q_send_own(True).wait_send())
    pl.when(blk > 0)(lambda: q_send_own(False).wait_send())
    for far in range(1, n_blk):
        pl.when((blk - far >= 0) & (blk < n_blk - 1))(lambda: q_copy(blk - far, True).wait_send())
        pl.when((blk + far <= n_blk - 1) & (blk > 0))(lambda: q_copy(blk + far, False).wait_send())
    for step in range(steps):
        o_copy(step, fac).wait_send()
        for distance in range(1, chips):
            y_copy(step, distance, grp).wait_send()
            c_copy(step, distance, other_chip(-distance)).wait_send()


def term_of(queries, factor, n_blk, n_fac):
    n_queries, n_rows = queries.shape[0], factor.shape[0]
    dims = factor.shape[1] * n_fac
    steps = n_rows // STEP_ROWS
    far_steps = steps * (n_fac // CORES - 1)
    dma = pltpu.SemaphoreType.DMA
    pairs = [far_steps] * 4 + [steps] * 2 + [far_steps] * 2
    return pl.pallas_call(
        functools.partial(term_kernel, n_blk, n_fac),
        out_shape=jax.ShapeDtypeStruct((n_queries, dims), jnp.bfloat16),
        in_specs=[pl.BlockSpec(memory_space=pl.ANY)] * 2,
        out_specs=pl.BlockSpec(memory_space=pltpu.VMEM),
        scratch_shapes=[
            pltpu.VMEM((n_queries, dims), jnp.bfloat16),
            pltpu.VMEM((n_rows, dims), jnp.bfloat16),
            pltpu.VMEM((n_queries, dims), jnp.float32),
            dma((2,)),
            dma((n_blk + 2,)),
            dma((n_blk,)),
        ]
        + [dma((count,)) for count in pairs],
        compiler_params=pltpu.CompilerParams(
            collective_id=0, has_side_effects=True, vmem_limit_bytes=56 * 2**20
        ),
    )(queries, factor)


def score_kernel(n_blk, term, train, scores, sums, precond, grads, load_sem, *sems):
    blk = lax.axis_index("blk")
    dims = term.shape[1]
    count = dims // 2 // CHUNK
    up_sum, down_sum, up_share, down_share = (
        (sems[2 * k], sems[2 * k + 1]) for k in range(4)
    )
    meet([{"blk": (blk + 1) % n_blk}, {"blk": (blk + n_blk - 1) % n_blk}])
    load = pltpu.make_async_copy(train, grads, load_sem)
    load.start()
    scores[...] = jnp.zeros_like(scores)

    flows = (
        (blk, {"blk": blk + 1}, {"blk": blk - 1}, 0, up_sum, up_share),
        (n_blk - 1 - blk, {"blk": blk - 1}, {"blk": blk + 1}, dims // 2, down_sum, down_share),
    )
    last = n_blk - 1

    def chunk(base, i):
        return (slice(None), at_multiple(base + i * CHUNK, CHUNK))

    def sum_copy(flow, i, first=False):
        _, ahead, _, base, sum_sems, _ = flow
        here = chunk(base, i)
        return remote((term if first else sums).at[here], sums.at[here], sum_sems, i, ahead)

    def share_copy(flow, i):
        _, _, back, base, _, share_sems = flow
        part = precond.at[chunk(base, i)]
        return remote(part, part, share_sems, i, back)

    def add(flow, i):
        place, base = flow[0], flow[3]
        here = chunk(base, i)

        @pl.when(place == 0)
        def _():
            sum_copy(flow, i, True).start()

        @pl.when(place > 0)
        def _():
            sum_copy(flow, i).wait_recv()
            added = sums[here].astype(jnp.float32) + term[here].astype(jnp.float32)
            added = added.astype(jnp.bfloat16)

            @pl.when(place < last)
            def _():
                sums[here] = added
                sum_copy(flow, i).start()

            @pl.when(place == last)
            def _():
                precond[here] = added
                share_copy(flow, i).start()

    def use(flow, i):
        place, base = flow[0], flow[3]

        @pl.when(place < last)
        def _():
            share_copy(flow, i).wait_recv()
            pl.when(place > 0)(lambda: share_copy(flow, i).start())

        @pl.when(i % 2 == 1)
        def _():
            cols = at_multiple(base + (i // 2) * (2 * CHUNK), 2 * CHUNK)
            scores[...] += contract_last(grads[:, cols], precond[:, cols])

    def turn(t, with_use):
        for flow in flows:
            i = t - flow[0] * HOP
            pl.when((i >= 0) & (i < count))(functools.partial(add, flow, i))
        if with_use:
            for flow in flows:
                i = t - (2 * last - flow[0]) * HOP
                pl.when((i >= 0) & (i < count))(functools.partial(use, flow, i))

    @pl.loop(0, last * HOP)
    def _(t):
        turn(t, False)

    load.wait()

    @pl.loop(last * HOP, count + 2 * last * HOP)
    def _(t):
        turn(t, True)

    for flow in flows:
        place = flow[0]

        @pl.loop(0, count)
        def _(i):
            pl.when(place < last)(lambda: sum_copy(flow, i).wait_send())
            pl.when(place > 0)(lambda: share_copy(flow, i).wait_send())


def scores_of(term, train, n_blk):
    dma = pltpu.SemaphoreType.DMA
    count = term.shape[1] // 2 // CHUNK
    return pl.pallas_call(
        functools.partial(score_kernel, n_blk),
        out_shape=jax.ShapeDtypeStruct((train.shape[0], term.shape[0]), jnp.float32),
        in_specs=[pl.BlockSpec(memory_space=pltpu.VMEM), pl.BlockSpec(memory_space=pl.ANY)],
        out_specs=pl.BlockSpec(memory_space=pltpu.VMEM),
        scratch_shapes=[
            pltpu.VMEM(term.shape, jnp.bfloat16),
            pltpu.VMEM(term.shape, jnp.bfloat16),
            pltpu.VMEM(train.shape, jnp.bfloat16),
            dma(()),
        ]
        + [dma((count,))] * 8,
        compiler_params=pltpu.CompilerParams(
            collective_id=1, has_side_effects=True, vmem_limit_bytes=48 * 2**20
        ),
    )(term, train)


def solution(mesh):
    n_blk, n_fac = mesh.shape["blk"], mesh.shape["fac"]

    def shards(train_grads, queries, factor):
        term = term_of(queries, factor, n_blk, n_fac)
        return scores_of(term, train_grads, n_blk)

    placed = (P(("grp", "blk"), None), P(("grp", "fac"), "blk"), P("blk", "fac"))
    return jax.shard_map(
        shards, mesh=mesh, in_specs=placed, out_specs=P(("grp", "blk"), "fac"), check_vma=False
    )
```

```python
import functools

import jax
import jax.numpy as jnp
from jax import lax
from jax.experimental import pallas as pl
from jax.experimental.pallas import tpu as pltpu
from jax.sharding import PartitionSpec as P

MESH = pl.DeviceIdType.MESH
CORES = 2
SLABS = 4
HOP = 2
CHUNK = 256

contract_last = functools.partial(
    lax.dot_general,
    dimension_numbers=(((1,), (1,)), ((), ())),
    preferred_element_type=jnp.float32,
)


def at_multiple(start, size):
    return pl.ds(pl.multiple_of(start, size), size)


def remote(src, dst, sems, index, target):
    send_sems, recv_sems = sems
    return pltpu.make_async_remote_copy(
        src_ref=src,
        dst_ref=dst,
        send_sem=send_sems.at[index],
        recv_sem=recv_sems.at[index],
        device_id=target,
        device_id_type=MESH,
    )


def meet(targets):
    barrier = pltpu.get_barrier_semaphore()
    for target in targets:
        pl.semaphore_signal(barrier, inc=1, device_id=target, device_id_type=MESH)
    pl.semaphore_wait(barrier, len(targets))


def kernel(
    n_blk, n_fac, train, queries, factor, scores,
    weights, whole, mixing, partial, arrived, mixed, term, sums, precond, grads, found, others,
    gathered, local_sems, *sems,
):
    blk, fac = lax.axis_index("blk"), lax.axis_index("fac")
    chips = n_fac // CORES
    chip, core = fac // CORES, fac % CORES
    n_rows, width = factor.shape
    n_queries, q_width = queries.shape
    span = CORES * width
    share = n_queries // SLABS
    slab = chips * share
    pairs = [(sems[2 * k], sems[2 * k + 1]) for k in range(len(sems) // 2)]
    q_sems, f_sems, a_sems, b_sems, s_sems, up_sum, down_sum, up_share, down_share = pairs
    last = n_blk - 1

    def other_chip(distance):
        return (chip + distance + chips) % chips

    def device_of(place):
        return {"fac": place * CORES + core}

    beside = {"fac": chip * CORES + 1 - core}
    far_chips = range(1, chips)
    meet(
        [beside]
        + [device_of(other_chip(distance)) for distance in far_chips]
        + [{"blk": (blk + 1) % n_blk}, {"blk": (blk + last) % n_blk}]
    )

    def q_part(owner, k):
        return whole.at[at_multiple(k * share, share), at_multiple(owner * q_width, q_width)]

    def q_own(k, up):
        return pltpu.make_async_remote_copy(
            src_ref=queries.at[at_multiple(k * share, share), :],
            dst_ref=q_part(blk, k),
            send_sem=q_sems[0].at[(n_blk if up else n_blk + 1) * SLABS + k],
            recv_sem=q_sems[1].at[blk * SLABS + k],
            device_id={"blk": blk + 1 if up else blk - 1},
            device_id_type=MESH,
        )

    def q_relay(owner, k, up):
        part = q_part(owner, k)
        return remote(part, part, q_sems, owner * SLABS + k, {"blk": blk + 1 if up else blk - 1})

    def own_queries(k):
        pl.when(blk < last)(lambda: q_own(k, True).start())
        pl.when(blk > 0)(lambda: q_own(k, False).start())

    def relay(k, far):
        @pl.when(blk - far >= 0)
        def _():
            q_relay(blk - far, k, True).wait_recv()
            pl.when(blk < last)(lambda: q_relay(blk - far, k, True).start())

        @pl.when(blk + far <= last)
        def _():
            q_relay(blk + far, k, False).wait_recv()
            pl.when(blk > 0)(lambda: q_relay(blk + far, k, False).start())

    def columns_of(owner_core):
        return weights.at[:, at_multiple(owner_core * width, width)]

    def f_copy(owner_core):
        return remote(factor, columns_of(owner_core), f_sems, 0, beside)

    def a_copy(k, distance, source):
        to = other_chip(distance)
        return remote(
            whole.at[at_multiple(k * share, share), at_multiple(to * span, span)],
            mixing.at[at_multiple(k * slab + source * share, share), :],
            a_sems,
            (distance - 1) * SLABS + k,
            device_of(to),
        )

    def b_copy(k, distance):
        here = at_multiple(k * slab, slab)
        return remote(
            partial.at[here, :],
            arrived.at[distance - 1, here, :],
            b_sems,
            (distance - 1) * SLABS + k,
            device_of(other_chip(distance)),
        )

    def s_copy(k, distance):
        to = other_chip(distance)
        return remote(
            found.at[at_multiple(k * slab + to * share, share), :],
            others.at[distance - 1, at_multiple(k * share, share), :],
            s_sems,
            (distance - 1) * SLABS + k,
            device_of(to),
        )

    keep_factor = pltpu.make_async_copy(factor, columns_of(core), local_sems.at[0])
    keep_queries = pltpu.make_async_copy(
        queries, whole.at[:, at_multiple(blk * q_width, q_width)], local_sems.at[1]
    )
    keep_grads = pltpu.make_async_copy(
        train.at[:, at_multiple(chip * span, span)], grads, local_sems.at[2]
    )

    def exchange_queries(k):
        for distance in far_chips:
            a_copy(k, distance, chip).start()
        mixing[at_multiple(k * slab + chip * share, share), :] = whole[
            at_multiple(k * share, share), at_multiple(chip * span, span)
        ]

    def mix(k):
        for distance in far_chips:
            a_copy(k, distance, other_chip(-distance)).wait_recv()
        here = at_multiple(k * slab, slab)
        tile = min(256, n_rows)

        @pl.loop(0, n_rows // tile)
        def _(j):
            at = at_multiple(j * tile, tile)
            partial[here, at] = contract_last(mixing[here, :], weights[at, :]).astype(jnp.bfloat16)

        for distance in far_chips:
            b_copy(k, distance).start()

    def make_term(k):
        here = at_multiple(k * slab, slab)
        total = partial[here, :].astype(jnp.float32)
        for distance in far_chips:
            b_copy(k, distance).wait_recv()
            total = total + arrived[distance - 1, here, :].astype(jnp.float32)
        mixed[...] = total.astype(jnp.bfloat16)
        tile = min(512, span)

        @pl.loop(0, span // tile)
        def _(j):
            at = at_multiple(j * tile, tile)
            term[here, at] = jnp.dot(
                mixed[...], weights[:, at], preferred_element_type=jnp.float32
            ).astype(jnp.bfloat16)

    half = span // 2
    per_slab = half // CHUNK
    count = SLABS * per_slab
    flows = (
        (blk, {"blk": blk + 1}, {"blk": blk - 1}, 0, up_sum, up_share),
        (last - blk, {"blk": blk - 1}, {"blk": blk + 1}, half, down_sum, down_share),
    )

    def chunk(base, i, parts=1):
        start = base + (i % per_slab) // parts * parts * CHUNK
        return (
            at_multiple(i // per_slab * slab, slab),
            at_multiple(start, parts * CHUNK),
        )

    def sum_copy(flow, i, first=False):
        _, ahead, _, base, sum_sems, _ = flow
        here = chunk(base, i)
        return remote((term if first else sums).at[here], sums.at[here], sum_sems, i, ahead)

    def share_copy(flow, i):
        _, _, back, base, _, share_sems = flow
        part = precond.at[chunk(base, i)]
        return remote(part, part, share_sems, i, back)

    def add(flow, i):
        place, base = flow[0], flow[3]
        here = chunk(base, i)

        @pl.when(place == 0)
        def _():
            sum_copy(flow, i, True).start()

        @pl.when(place > 0)
        def _():
            sum_copy(flow, i).wait_recv()
            added = sums[here].astype(jnp.float32) + term[here].astype(jnp.float32)
            added = added.astype(jnp.bfloat16)

            @pl.when(place < last)
            def _():
                sums[here] = added
                sum_copy(flow, i).start()

            @pl.when(place == last)
            def _():
                precond[here] = added
                share_copy(flow, i).start()

    def use(flow, i):
        place, base = flow[0], flow[3]

        @pl.when(place < last)
        def _():
            share_copy(flow, i).wait_recv()
            pl.when(place > 0)(lambda: share_copy(flow, i).start())

        @pl.when(i % 2 == 1)
        def _():
            rows, cols = chunk(base, i, 2)
            found[rows, :] += contract_last(precond[rows, cols], grads[:, cols])

    def turn(t):
        for flow in flows:
            i = t - flow[0] * HOP
            pl.when((i >= 0) & (i < count))(functools.partial(add, flow, i))
        for flow in flows:
            i = t - (2 * last - flow[0]) * HOP
            pl.when((i >= 0) & (i < count))(functools.partial(use, flow, i))

    def send_found(k):
        for distance in far_chips:
            s_copy(k, distance).start()

    own_queries(0)
    f_copy(core).start()
    own_queries(1)
    keep_queries.start()
    keep_factor.start()
    keep_grads.start()
    found[...] = jnp.zeros_like(found)
    for k in range(SLABS):
        for far in range(1, n_blk):
            relay(k, far)
        if k + 2 < SLABS:
            own_queries(k + 2)
        if k == 0:
            keep_queries.wait()
        exchange_queries(k)
        if k == 1:
            keep_factor.wait()
            f_copy(1 - core).wait_recv()
        if 1 <= k < SLABS - 1:
            mix(k - 1)
        if 2 <= k < SLABS - 1:
            make_term(k - 2)
    keep_grads.wait()

    lag = 2 * last * HOP
    tasks = [
        (per_slab // 2, mix, SLABS - 2),
        (per_slab - 1, make_term, SLABS - 3),
        (per_slab + per_slab // 4, mix, SLABS - 1),
        (2 * per_slab - 2, make_term, SLABS - 2),
        (3 * per_slab - 3, make_term, SLABS - 1),
    ] + [((k + 1) * per_slab + lag, send_found, k) for k in range(SLABS)]
    begin = 0
    for end, task, k in sorted(tasks, key=lambda entry: entry[0]):
        if end > begin:
            pl.loop(begin, end)(turn)
            begin = end
        task(k)

    for k in range(SLABS):
        total = found[at_multiple(k * slab + chip * share, share), :]
        for distance in far_chips:
            s_copy(k, distance).wait_recv()
            total = total + others[distance - 1, k * share : (k + 1) * share, :]
        gathered[k * share : (k + 1) * share, :] = total
    scores[...] = gathered[...].T

    f_copy(core).wait_send()
    for k in range(SLABS):
        pl.when(blk < last)(lambda: q_own(k, True).wait_send())
        pl.when(blk > 0)(lambda: q_own(k, False).wait_send())
        for far in range(1, n_blk):
            pl.when((blk - far >= 0) & (blk < last))(
                lambda: q_relay(blk - far, k, True).wait_send()
            )
            pl.when((blk + far <= last) & (blk > 0))(
                lambda: q_relay(blk + far, k, False).wait_send()
            )
        for distance in far_chips:
            a_copy(k, distance, chip).wait_send()
            b_copy(k, distance).wait_send()
            s_copy(k, distance).wait_send()
    for flow in flows:
        place = flow[0]

        @pl.loop(0, count)
        def _(i):
            pl.when(place < last)(lambda: sum_copy(flow, i).wait_send())
            pl.when(place > 0)(lambda: share_copy(flow, i).wait_send())


def solution(mesh):
    n_blk, n_fac = mesh.shape["blk"], mesh.shape["fac"]
    chips = n_fac // CORES

    def shards(train_grads, queries, factor):
        examples, dims = train_grads.shape
        n_rows, width = factor.shape
        n_queries = queries.shape[0]
        span, many = CORES * width, chips * n_queries
        chunks = SLABS * (span // 2 // CHUNK)
        far = (chips - 1) * SLABS
        dma, bf16, f32 = pltpu.SemaphoreType.DMA, jnp.bfloat16, jnp.float32
        counts = [(n_blk + 2) * SLABS, n_blk * SLABS, 1, 1] + [far] * 6 + [chunks] * 8
        return pl.pallas_call(
            functools.partial(kernel, n_blk, n_fac),
            out_shape=jax.ShapeDtypeStruct((examples, n_queries), f32),
            in_specs=[pl.BlockSpec(memory_space=pl.ANY)] * 3,
            out_specs=pl.BlockSpec(memory_space=pltpu.VMEM),
            scratch_shapes=[
                pltpu.VMEM((n_rows, span), bf16),
                pltpu.VMEM((n_queries, dims), bf16),
                pltpu.VMEM((many, span), bf16),
                pltpu.VMEM((many, n_rows), bf16),
                pltpu.VMEM((chips - 1, many, n_rows), bf16),
                pltpu.VMEM((many // SLABS, n_rows), bf16),
                pltpu.VMEM((many, span), bf16),
                pltpu.VMEM((many, span), bf16),
                pltpu.VMEM((many, span), bf16),
                pltpu.VMEM((examples, span), bf16),
                pltpu.VMEM((many, examples), f32),
                pltpu.VMEM((chips - 1, n_queries, examples), f32),
                pltpu.VMEM((n_queries, examples), f32),
                dma((3,)),
            ]
            + [dma((size,)) for size in counts],
            compiler_params=pltpu.CompilerParams(
                collective_id=0, has_side_effects=True, vmem_limit_bytes=58 * 2**20
            ),
        )(train_grads, queries, factor)

    placed = (P(("grp", "blk"), None), P(("grp", "fac"), "blk"), P("blk", "fac"))
    return jax.shard_map(
        shards, mesh=mesh, in_specs=placed, out_specs=P(("grp", "blk"), "fac"), check_vma=False
    )
```

```python
import functools

import jax
import jax.numpy as jnp
from jax import lax
from jax.experimental import pallas as pl
from jax.experimental.pallas import tpu as pltpu
from jax.sharding import PartitionSpec as P

MESH = pl.DeviceIdType.MESH
CORES = 2
SLABS = 4
HOP = 2
CHUNK = 256

contract_last = functools.partial(
    lax.dot_general,
    dimension_numbers=(((1,), (1,)), ((), ())),
    preferred_element_type=jnp.float32,
)


def at_multiple(start, size):
    return pl.ds(pl.multiple_of(start, size), size)


def remote(src, dst, sems, index, target):
    send_sems, recv_sems = sems
    return pltpu.make_async_remote_copy(
        src_ref=src,
        dst_ref=dst,
        send_sem=send_sems.at[index],
        recv_sem=recv_sems.at[index],
        device_id=target,
        device_id_type=MESH,
    )


def meet(targets):
    barrier = pltpu.get_barrier_semaphore()
    for target in targets:
        pl.semaphore_signal(barrier, inc=1, device_id=target, device_id_type=MESH)
    pl.semaphore_wait(barrier, len(targets))


def kernel(
    n_blk, n_fac, train, queries, factor, scores,
    weights, whole, mixing, partial, arrived, mixed, term, sums, precond, grads, found, others,
    gathered, local_sems, *sems,
):
    blk, fac = lax.axis_index("blk"), lax.axis_index("fac")
    chips = n_fac // CORES
    chip, core = fac // CORES, fac % CORES
    n_rows, width = factor.shape
    n_queries, q_width = queries.shape
    span = CORES * width
    share = n_queries // SLABS
    slab = chips * share
    pairs = [(sems[2 * k], sems[2 * k + 1]) for k in range(len(sems) // 2)]
    q_sems, f_sems, a_sems, b_sems, s_sems, up_sum, down_sum, up_share, down_share = pairs
    last = n_blk - 1

    def other_chip(distance):
        return (chip + distance + chips) % chips

    def device_of(place):
        return {"fac": place * CORES + core}

    beside = {"fac": chip * CORES + 1 - core}
    far_chips = range(1, chips)
    meet(
        [beside]
        + [device_of(other_chip(distance)) for distance in far_chips]
        + [{"blk": (blk + 1) % n_blk}, {"blk": (blk + last) % n_blk}]
    )

    def q_part(owner, k):
        return whole.at[at_multiple(k * share, share), at_multiple(owner * q_width, q_width)]

    def q_own(k, up):
        return pltpu.make_async_remote_copy(
            src_ref=queries.at[at_multiple(k * share, share), :],
            dst_ref=q_part(blk, k),
            send_sem=q_sems[0].at[(n_blk if up else n_blk + 1) * SLABS + k],
            recv_sem=q_sems[1].at[blk * SLABS + k],
            device_id={"blk": blk + 1 if up else blk - 1},
            device_id_type=MESH,
        )

    def q_relay(owner, k, up):
        part = q_part(owner, k)
        return remote(part, part, q_sems, owner * SLABS + k, {"blk": blk + 1 if up else blk - 1})

    def own_queries(k):
        pl.when(blk < last)(lambda: q_own(k, True).start())
        pl.when(blk > 0)(lambda: q_own(k, False).start())

    def relay(k, far):
        @pl.when(blk - far >= 0)
        def _():
            q_relay(blk - far, k, True).wait_recv()
            pl.when(blk < last)(lambda: q_relay(blk - far, k, True).start())

        @pl.when(blk + far <= last)
        def _():
            q_relay(blk + far, k, False).wait_recv()
            pl.when(blk > 0)(lambda: q_relay(blk + far, k, False).start())

    def columns_of(owner_core):
        return weights.at[:, at_multiple(owner_core * width, width)]

    def f_copy(owner_core):
        return remote(factor, columns_of(owner_core), f_sems, 0, beside)

    def a_copy(k, distance, source):
        to = other_chip(distance)
        return remote(
            whole.at[at_multiple(k * share, share), at_multiple(to * span, span)],
            mixing.at[at_multiple(k * slab + source * share, share), :],
            a_sems,
            (distance - 1) * SLABS + k,
            device_of(to),
        )

    def b_copy(k, distance):
        here = at_multiple(k * slab, slab)
        return remote(
            partial.at[here, :],
            arrived.at[distance - 1, here, :],
            b_sems,
            (distance - 1) * SLABS + k,
            device_of(other_chip(distance)),
        )

    def s_copy(k, distance):
        to = other_chip(distance)
        return remote(
            found.at[at_multiple(k * slab + to * share, share), :],
            others.at[distance - 1, at_multiple(k * share, share), :],
            s_sems,
            (distance - 1) * SLABS + k,
            device_of(to),
        )

    keep_factor = pltpu.make_async_copy(factor, columns_of(core), local_sems.at[0])
    keep_queries = pltpu.make_async_copy(
        queries, whole.at[:, at_multiple(blk * q_width, q_width)], local_sems.at[1]
    )
    keep_grads = pltpu.make_async_copy(
        train.at[:, at_multiple(chip * span, span)], grads, local_sems.at[2]
    )

    def exchange_queries(k):
        for distance in far_chips:
            a_copy(k, distance, chip).start()
        mixing[at_multiple(k * slab + chip * share, share), :] = whole[
            at_multiple(k * share, share), at_multiple(chip * span, span)
        ]

    def mix(k):
        here = at_multiple(k * slab, slab)
        tile = min(256, n_rows)

        def before():
            for distance in far_chips:
                a_copy(k, distance, other_chip(-distance)).wait_recv()

        def one(j):
            at = at_multiple(j * tile, tile)
            partial[here, at] = contract_last(mixing[here, :], weights[at, :]).astype(jnp.bfloat16)

        def after():
            for distance in far_chips:
                b_copy(k, distance).start()

        return before, one, n_rows // tile, after

    def make_term(k):
        here = at_multiple(k * slab, slab)
        tile = min(512, span)

        def before():
            total = partial[here, :].astype(jnp.float32)
            for distance in far_chips:
                b_copy(k, distance).wait_recv()
                total = total + arrived[distance - 1, here, :].astype(jnp.float32)
            mixed[...] = total.astype(jnp.bfloat16)

        def one(j):
            at = at_multiple(j * tile, tile)
            term[here, at] = jnp.dot(
                mixed[...], weights[:, at], preferred_element_type=jnp.float32
            ).astype(jnp.bfloat16)

        return before, one, span // tile, lambda: None

    def at_once(work):
        before, one, tiles, after = work
        before()
        pl.loop(0, tiles)(one)
        after()

    half = span // 2
    per_slab = half // CHUNK
    count = SLABS * per_slab
    flows = (
        (blk, {"blk": blk + 1}, {"blk": blk - 1}, 0, up_sum, up_share),
        (last - blk, {"blk": blk - 1}, {"blk": blk + 1}, half, down_sum, down_share),
    )

    def chunk(base, i, parts=1):
        start = base + (i % per_slab) // parts * parts * CHUNK
        return (
            at_multiple(i // per_slab * slab, slab),
            at_multiple(start, parts * CHUNK),
        )

    def sum_copy(flow, i, first=False):
        _, ahead, _, base, sum_sems, _ = flow
        here = chunk(base, i)
        return remote((term if first else sums).at[here], sums.at[here], sum_sems, i, ahead)

    def share_copy(flow, i):
        _, _, back, base, _, share_sems = flow
        part = precond.at[chunk(base, i)]
        return remote(part, part, share_sems, i, back)

    def add(flow, i):
        place, base = flow[0], flow[3]
        here = chunk(base, i)

        @pl.when(place == 0)
        def _():
            sum_copy(flow, i, True).start()

        @pl.when(place > 0)
        def _():
            sum_copy(flow, i).wait_recv()
            added = sums[here].astype(jnp.float32) + term[here].astype(jnp.float32)
            added = added.astype(jnp.bfloat16)

            @pl.when(place < last)
            def _():
                sums[here] = added
                sum_copy(flow, i).start()

            @pl.when(place == last)
            def _():
                precond[here] = added
                share_copy(flow, i).start()

    def use(flow, i):
        place, base = flow[0], flow[3]

        @pl.when(place < last)
        def _():
            share_copy(flow, i).wait_recv()
            pl.when(place > 0)(lambda: share_copy(flow, i).start())

        @pl.when(i % 2 == 1)
        def _():
            rows, cols = chunk(base, i, 2)
            found[rows, :] += contract_last(precond[rows, cols], grads[:, cols])

    def turn(t):
        for flow in flows:
            i = t - flow[0] * HOP
            pl.when((i >= 0) & (i < count))(functools.partial(add, flow, i))
        for flow in flows:
            i = t - (2 * last - flow[0]) * HOP
            pl.when((i >= 0) & (i < count))(functools.partial(use, flow, i))

    def send_found(k):
        for distance in far_chips:
            s_copy(k, distance).start()

    own_queries(0)
    f_copy(core).start()
    own_queries(1)
    keep_queries.start()
    keep_factor.start()
    keep_grads.start()
    found[...] = jnp.zeros_like(found)
    for k in range(SLABS):
        for far in range(1, n_blk):
            relay(k, far)
        if k + 2 < SLABS:
            own_queries(k + 2)
        if k == 0:
            keep_queries.wait()
        exchange_queries(k)
        if k == 1:
            keep_factor.wait()
            f_copy(1 - core).wait_recv()
        if 1 <= k < SLABS - 1:
            at_once(mix(k - 1))
        if 2 <= k < SLABS - 1:
            at_once(make_term(k - 2))
    keep_grads.wait()

    def turns(begin, end, work=None):
        if work is None:
            pl.loop(begin, end)(turn)
            return
        before, one, tiles, after = work
        each = -(-tiles // (end - begin))
        before()

        @pl.loop(begin, end)
        def _(t):
            turn(t)
            for extra in range(each):
                j = (t - begin) * each + extra
                if each * (end - begin) == tiles:
                    one(j)
                else:
                    pl.when(j < tiles)(functools.partial(one, j))

        after()

    lag = 2 * last * HOP
    part = per_slab // 2
    turns(0, part, mix(SLABS - 2))
    turns(part, 2 * part, make_term(SLABS - 3))
    turns(2 * part, 3 * part, mix(SLABS - 1))
    turns(3 * part, 4 * part, make_term(SLABS - 2))
    turns(4 * part, 5 * part)
    turns(5 * part, 6 * part, make_term(SLABS - 1))
    begin = 6 * part
    for k in range(SLABS):
        end = (k + 1) * per_slab + lag
        if end > begin:
            turns(begin, end)
            begin = end
        send_found(k)

    for k in range(SLABS):
        total = found[at_multiple(k * slab + chip * share, share), :]
        for distance in far_chips:
            s_copy(k, distance).wait_recv()
            total = total + others[distance - 1, k * share : (k + 1) * share, :]
        gathered[k * share : (k + 1) * share, :] = total
    scores[...] = gathered[...].T

    f_copy(core).wait_send()
    for k in range(SLABS):
        pl.when(blk < last)(lambda: q_own(k, True).wait_send())
        pl.when(blk > 0)(lambda: q_own(k, False).wait_send())
        for far in range(1, n_blk):
            pl.when((blk - far >= 0) & (blk < last))(
                lambda: q_relay(blk - far, k, True).wait_send()
            )
            pl.when((blk + far <= last) & (blk > 0))(
                lambda: q_relay(blk + far, k, False).wait_send()
            )
        for distance in far_chips:
            a_copy(k, distance, chip).wait_send()
            b_copy(k, distance).wait_send()
            s_copy(k, distance).wait_send()
    for flow in flows:
        place = flow[0]

        @pl.loop(0, count)
        def _(i):
            pl.when(place < last)(lambda: sum_copy(flow, i).wait_send())
            pl.when(place > 0)(lambda: share_copy(flow, i).wait_send())


def solution(mesh):
    n_blk, n_fac = mesh.shape["blk"], mesh.shape["fac"]
    chips = n_fac // CORES

    def shards(train_grads, queries, factor):
        examples, dims = train_grads.shape
        n_rows, width = factor.shape
        n_queries = queries.shape[0]
        span, many = CORES * width, chips * n_queries
        chunks = SLABS * (span // 2 // CHUNK)
        far = (chips - 1) * SLABS
        dma, bf16, f32 = pltpu.SemaphoreType.DMA, jnp.bfloat16, jnp.float32
        counts = [(n_blk + 2) * SLABS, n_blk * SLABS, 1, 1] + [far] * 6 + [chunks] * 8
        return pl.pallas_call(
            functools.partial(kernel, n_blk, n_fac),
            out_shape=jax.ShapeDtypeStruct((examples, n_queries), f32),
            in_specs=[pl.BlockSpec(memory_space=pl.ANY)] * 3,
            out_specs=pl.BlockSpec(memory_space=pltpu.VMEM),
            scratch_shapes=[
                pltpu.VMEM((n_rows, span), bf16),
                pltpu.VMEM((n_queries, dims), bf16),
                pltpu.VMEM((many, span), bf16),
                pltpu.VMEM((many, n_rows), bf16),
                pltpu.VMEM((chips - 1, many, n_rows), bf16),
                pltpu.VMEM((many // SLABS, n_rows), bf16),
                pltpu.VMEM((many, span), bf16),
                pltpu.VMEM((many, span), bf16),
                pltpu.VMEM((many, span), bf16),
                pltpu.VMEM((examples, span), bf16),
                pltpu.VMEM((many, examples), f32),
                pltpu.VMEM((chips - 1, n_queries, examples), f32),
                pltpu.VMEM((n_queries, examples), f32),
                dma((3,)),
            ]
            + [dma((size,)) for size in counts],
            compiler_params=pltpu.CompilerParams(
                collective_id=0, has_side_effects=True, vmem_limit_bytes=58 * 2**20
            ),
        )(train_grads, queries, factor)

    placed = (P(("grp", "blk"), None), P(("grp", "fac"), "blk"), P("blk", "fac"))
    return jax.shard_map(
        shards, mesh=mesh, in_specs=placed, out_specs=P(("grp", "blk"), "fac"), check_vma=False
    )
```
